32 devices in a mesh: seq: 16 (over z, y, core), kv: 2 (over x).
Axes of the slice: x: 2, y: 2, z: 4, core: 2. Of those that a mesh axis runs over, the one named last changes fastest.
Arguments:
- plan: int32 [16], replicated, may hold values from 0 to 15, each once
- queries: bfloat16 [2048, 1024], P('seq', 'kv'), may hold values from -24 to 24
- keys: bfloat16 [2048, 256], P('seq', 'kv'), may hold values from -9 to 9
- student_c: bfloat16 [2048, 1024], P('seq', 'kv'), may hold values from -0.125 to 0.125
- layer_input: bfloat16 [2048, 8192], P('seq', 'kv'), may hold values from -6 to 6
- b_weight: bfloat16 [2, 8192, 128], P('kv'), may hold values from -0.0625 to 0.0625
Outputs:
- grad_c: bfloat16 [2048, 1024], P('seq', 'kv')
- grad_wb: float32 [2, 8192, 128], P('kv', 'seq')
The draws below stay inside these ranges and needn't reach their ends.
Inputs may be any that keep to these rules, and one draw needn't show every extreme that they name: Each value appears once: plan[d] is the block of 128 consecutive positions held by index d of seq.
All inputs are finite; a program needn't handle non-finite values.
Results may differ from the reference program's by a relative error of at most 0.0049.
Values may be sent and summed in bfloat16 or wider, within the bound.
A program may use at most 64 MiB of HBM per device.

```python
import math
import jax
import jax.numpy as jnp
from jax import lax

D = 8192
N = 128
H = 4
TOK_DEV = 128
GROUPS = 2
TOKENS = 2048
N_SEQ = 16


def key_table(key):
    base = jax.random.fold_in(key, 101)
    raw = jnp.clip(jax.random.normal(jax.random.fold_in(base, 1), (TOKENS, GROUPS, N), jnp.float32), -4.0, 4.0)
    return raw


def draw_keys(key, part):
    raw = key_table(key)
    return raw.reshape(TOKENS, GROUPS * N).astype(jnp.bfloat16)


def draw_queries(key, part):
    base = jax.random.fold_in(key, 202)
    raw = 3.5 * jnp.clip(jax.random.normal(jax.random.fold_in(base, 1), (TOKENS, GROUPS, H, N), jnp.float32), -6.0, 6.0)
    return raw.reshape(TOKENS, GROUPS * H * N).astype(jnp.bfloat16)


def raised(values, key, source, target, shards_of, factor):
    def block_of(dim):
        return (jnp.arange(values.shape[dim]) // (values.shape[dim] // shards_of)).reshape((-1,) + (1,) * (values.ndim - 1 - dim))

    first = jax.random.permutation(key, shards_of)[block_of(target)]
    second = (block_of(target) + shards_of // 2) % shards_of
    return jnp.where((block_of(source) == first) | (block_of(source) == second), factor * values, values)


def steps_of(key, extent, cuts, smallest, high):
    level = 1.0
    for axis_at, shards_of in cuts:
        steps = jax.random.uniform(jax.random.fold_in(jax.random.fold_in(key, 6), axis_at), (shards_of,), jnp.float32, smallest / len(cuts), high / len(cuts))
        level = level * jnp.repeat(jnp.exp(steps), extent[axis_at] // shards_of).reshape((-1,) + (1,) * (len(extent) - 1 - axis_at))
    return level


def gaussian(key, shape, width, bound, shards=(), kind=jnp.bfloat16):
    gain = steps_of(key, shape, shards, -0.22, 0.18) if shards else 1.0
    entries = jax.random.normal(key, shape, jnp.float32) * width * gain
    return jnp.minimum(jnp.maximum(entries, -bound), bound).astype(kind)


def gaussian_with(stream_key, shape, scale, limit, split, heavy, held_as=jnp.bfloat16):
    array = scale * jax.random.normal(stream_key, shape, jnp.float32)
    if split:
        array = array * steps_of(stream_key, shape, split, -0.22, 0.18)
    return jnp.clip(raised(array, jax.random.fold_in(stream_key, 3), *heavy), -limit, limit).astype(held_as)


def setup_inputs(seed: int = 0) -> dict:
    seeds = jax.random.split(jax.random.key(seed), 7)
    plan = jax.random.permutation(seeds[0], N_SEQ).astype(jnp.int32)
    queries = draw_queries(jax.random.fold_in(seeds[6], 71), 0)
    keys = draw_keys(jax.random.fold_in(seeds[6], 71), 0)
    student_c = gaussian(seeds[3], (TOKENS, GROUPS * H * N), TOKENS ** -0.5, 0.125, ((0, 16), (1, 2)))
    layer_input = gaussian_with(seeds[4], (TOKENS, D), 1.0, 6.0, ((0, 16), (1, 2)), (0, 1, 16, 2.0))
    b_weight = gaussian(seeds[5], (GROUPS, D, N), D ** -0.5, 0.0625, ((0, 2),))
    return dict(plan=plan, queries=queries, keys=keys, student_c=student_c, layer_input=layer_input, b_weight=b_weight)


NEG_FILL = -1e+30

def reference(plan, queries, keys, student_c, layer_input, b_weight):
    token_ids = jnp.arange(TOKENS, dtype=jnp.int32)
    positions = plan[token_ids // TOK_DEV] * TOK_DEV + token_ids % TOK_DEV
    student_scale = 2.0 / math.sqrt(TOKENS)
    score_scale = 1.0 / math.sqrt(N)
    block_rows = math.gcd(TOKENS, 512)
    steps_count = TOKENS // block_rows
    query_groups = jnp.transpose(queries.reshape(TOKENS, GROUPS, H, N), (1, 0, 2, 3))
    c_groups = jnp.transpose(student_c.reshape(TOKENS, GROUPS, H, N), (1, 0, 2, 3))
    key_groups = jnp.transpose(keys.reshape(TOKENS, GROUPS, N), (1, 0, 2))

    def one_group(group_items):
        query_all, key_all, c_all, weight = group_items
        b_proj = jnp.dot(layer_input, weight, preferred_element_type=jnp.float32).astype(jnp.bfloat16)
        b_float = b_proj.astype(jnp.float32)
        k_float = key_all.astype(jnp.float32)

        def query_step(db_acc, block_index):
            first_row = (block_index * block_rows).astype(jnp.int32)
            query_block = lax.dynamic_slice_in_dim(query_all, first_row, block_rows, 0).astype(jnp.float32)
            c_block = lax.dynamic_slice_in_dim(c_all, first_row, block_rows, 0).astype(jnp.float32)
            query_pos = lax.dynamic_slice_in_dim(positions, first_row, block_rows, 0)
            visible = positions[None, None, :] <= query_pos[:, None, None]
            scores = jnp.einsum('qhd,kd->qhk', query_block, k_float) * score_scale
            scores = jnp.where(visible, scores, NEG_FILL)
            highest = lax.optimization_barrier(jnp.max(scores, axis=-1, keepdims=True))
            weights = jnp.where(visible, jnp.exp(scores - highest), 0.0)
            totals = lax.optimization_barrier(jnp.sum(weights, axis=-1, keepdims=True))
            teacher = weights / totals
            student = student_scale * jnp.einsum('qhd,kd->qhk', c_block, b_float)
            residual = jnp.where(visible, student - teacher, 0.0).astype(jnp.bfloat16)
            resid_f = residual.astype(jnp.float32)
            grad_block = jnp.einsum('qhk,kd->qhd', resid_f, b_float).astype(jnp.bfloat16)
            db_acc = db_acc + jnp.einsum('qhk,qhd->kd', resid_f, c_block)
            return (db_acc, grad_block)
        db_acc, grad_blocks = lax.scan(query_step, jnp.zeros((TOKENS, N), jnp.float32), jnp.arange(steps_count, dtype=jnp.int32))
        b_grad = db_acc.astype(jnp.bfloat16)
        weight_grad = jnp.dot(layer_input.T, b_grad, preferred_element_type=jnp.float32)
        return (grad_blocks.reshape(TOKENS, H, N), weight_grad)
    grads, weight_grads = lax.map(one_group, (query_groups, key_groups, c_groups, b_weight))
    grad_c = jnp.transpose(grads, (1, 0, 2, 3)).reshape(TOKENS, GROUPS * H * N)
    return (grad_c, weight_grads)
```

```python
import functools
import math

import jax
import jax.numpy as jnp
from jax import lax
from jax.experimental import pallas as pl
from jax.experimental.pallas import tpu as pltpu
from jax.sharding import PartitionSpec as P

NEG_FILL = -1e30
MESH = pl.DeviceIdType.MESH
CHUNKS = 4
BF16 = jnp.bfloat16
F32 = jnp.float32
NT = (((1,), (1,)), ((), ()))
TN = (((0,), (0,)), ((), ()))


def dot(a, b, dims=(((1,), (0,)), ((), ()))):
    return lax.dot_general(a, b, dims, preferred_element_type=F32)


def kernel(
    n_seq, n_kv, rows, width, heads,
    plan, q_ref, k_ref, c_ref, x_ref, w_ref,
    gc_ref, gw_ref,
    q_st, c_st, k_all, b_all, s_buf, top, tot, acc,
    wx, pbs, pbr, lt, db_all, dbs, snd, arr, db_own, dbg, fs, fr,
    k_sem, kr_sem, w_sem, wr_sem, pb_sem, x_sem, b_sem, br_sem, ds_sem, da_sem, dg_sem, f_sem, loc_sem,
):
    me, kv = lax.axis_index("seq"), lax.axis_index("kv")
    chips = n_seq // 2
    chip, core = me // 2, lax.rem(me, 2)
    sib = me + 1 - 2 * core
    per = n_seq // n_kv
    grp, pos = me // per, lax.rem(me, per)
    half = x_ref.shape[1]
    feat = half // per
    piece = half // 2
    step = piece // CHUNKS
    total = n_seq * n_kv
    wide = 2 * rows

    def blk(i, size=rows):
        return pl.ds(pl.multiple_of(i * size, size), size)

    def remote(src, dst, sems, i, j, dev):
        return pltpu.make_async_remote_copy(
            src_ref=src, dst_ref=dst, send_sem=sems.at[0, i], recv_sem=sems.at[1, j],
            device_id=dev, device_id_type=MESH,
        )

    barrier = pltpu.get_barrier_semaphore()
    flat = me * n_kv + kv

    def greet(d, carry):
        other = lax.rem(flat + d, total)
        pl.semaphore_signal(
            barrier, inc=1, device_id=(other // n_kv, lax.rem(other, n_kv)), device_id_type=MESH
        )
        return carry

    lax.fori_loop(1, total, greet, 0)
    pl.semaphore_wait(barrier, total - 1)

    def each(lo, hi, body):
        def run(i, carry):
            body(i)
            return carry

        lax.fori_loop(lo, hi, run, 0)

    def w_rows(i):
        return pl.ds(pl.multiple_of(core * piece + i * step, step), step)

    def w_copy(dk, i):
        other = lax.rem(kv + dk, n_kv)
        src = pl.ds(pl.multiple_of(other * half + core * piece + i * step, step), step)
        return remote(
            w_ref.at[0, src], wx.at[kv, w_rows(i)], w_sem, other * CHUNKS + i, kv * CHUNKS + i, (me, other)
        )

    def w_arrival(dk, i):
        other = lax.rem(kv + dk, n_kv)
        spot = wx.at[other, w_rows(i)]
        return remote(spot, spot, w_sem, other * CHUNKS + i, other * CHUNKS + i, (me, other))

    def w_relay(dk, i):
        other = lax.rem(kv + dk, n_kv)
        spot = wx.at[other, w_rows(i)]
        return remote(spot, spot, wr_sem, other * CHUNKS + i, other * CHUNKS + i, (sib, kv))

    for i in range(CHUNKS):
        for dk in range(1, n_kv):
            w_copy(dk, i).start()

    def direct(buf, sems, d):
        to = lax.rem(chip + d, chips)
        spot = buf.at[blk(me)]
        return remote(spot, spot, sems, to, chip, (2 * to + core, kv))

    def arrival(buf, sems, d):
        frm = lax.rem(chip + d, chips)
        spot = buf.at[blk(2 * frm + core)]
        return remote(spot, spot, sems, frm, frm, (2 * frm + core, kv))

    def relay(buf, sems, d):
        frm = lax.rem(chip + d, chips)
        spot = buf.at[blk(2 * frm + core)]
        return remote(spot, spot, sems, frm, frm, (sib, kv))

    def relayed(buf, sems, d):
        frm = lax.rem(chip + d, chips)
        spot = buf.at[blk(2 * frm + 1 - core)]
        return remote(spot, spot, sems, frm, frm, (sib, kv))

    def pass_on(buf, sems, rsems):
        def one(d):
            arrival(buf, sems, d).wait_recv()
            relay(buf, rsems, d).start()

        each(1, chips, one)
        each(0, chips, lambda d: relayed(buf, rsems, d).wait_recv())

    k_all[blk(me)] = k_ref[...]
    each(1, chips, lambda d: direct(k_all, k_sem, d).start())
    relay(k_all, kr_sem, 0).start()

    def x_copy(d):
        to = lax.rem(pos + d, per)
        cols = pl.ds(pl.multiple_of(to * feat, feat), feat)
        return remote(x_ref.at[:, cols], lt.at[blk(pos)], x_sem, to, pos, (grp * per + to, kv))

    def x_arrival(d):
        frm = lax.rem(pos + d, per)
        spot = lt.at[blk(frm)]
        return remote(spot, spot, x_sem, frm, frm, (grp * per + frm, kv))

    each(1, per, lambda d: x_copy(d).start())
    own_cols = pl.ds(pl.multiple_of(pos * feat, feat), feat)
    mine = pltpu.make_async_copy(x_ref.at[:, own_cols], lt.at[blk(pos)], loc_sem)
    mine.start()

    for h in range(heads):
        q_st[h * rows:(h + 1) * rows, :] = q_ref[:, h * width:(h + 1) * width]
        c_st[h * rows:(h + 1) * rows, :] = c_ref[:, h * width:(h + 1) * width]
    pbr[kv] = dot(x_ref[...], w_ref[0, pl.ds(pl.multiple_of(kv * half, half), half)])

    pass_on(k_all, k_sem, kr_sem)

    def w_forward(i):
        for dk in range(1, n_kv):
            w_arrival(dk, i).wait_recv()
            w_relay(dk, i).start()

    w_forward(0)

    own_plan = plan[me]
    row_id = lax.broadcasted_iota(jnp.int32, (heads * rows, rows), 0)
    col_id = lax.broadcasted_iota(jnp.int32, (heads * rows, rows), 1)
    gap = col_id - lax.rem(row_id, rows)

    def seen(block):
        return gap <= (own_plan - plan[block]) * rows

    score_scale = 1.0 / math.sqrt(width)
    student_scale = 2.0 / math.sqrt(rows * n_seq)
    top[...] = jnp.full_like(top, NEG_FILL)

    def scores(i):
        both = dot(q_st[...], k_all[blk(i, wide)], NT) * score_scale
        high = top[...]
        for t in range(2):
            part = jnp.where(seen(2 * i + t), both[:, t * rows:(t + 1) * rows], NEG_FILL)
            s_buf[i, :, t * rows:(t + 1) * rows] = part
            high = jnp.maximum(high, part)
        top[...] = high

    each(0, chips, scores)
    top[...] = jnp.broadcast_to(jnp.max(top[...], axis=1, keepdims=True), top.shape)
    for i in range(1, CHUNKS - 1):
        w_forward(i)
    tot[...] = jnp.zeros_like(tot)

    def weights(i):
        added = tot[...]
        for t in range(2):
            part = jnp.exp(s_buf[i, :, t * rows:(t + 1) * rows] - top[...])
            s_buf[i, :, t * rows:(t + 1) * rows] = part
            added = added + part
        tot[...] = added

    each(0, chips, weights)
    w_forward(CHUNKS - 1)
    tot[...] = jnp.broadcast_to(1.0 / jnp.sum(tot[...], axis=1, keepdims=True), tot.shape)

    def relayed_w(dk, i):
        other = lax.rem(kv + dk, n_kv)
        spot = wx.at[other, pl.ds(pl.multiple_of((1 - core) * piece + i * step, step), step)]
        return remote(spot, spot, wr_sem, other * CHUNKS + i, other * CHUNKS + i, (sib, kv))

    def pb_copy(dk):
        other = lax.rem(kv + dk, n_kv)
        return remote(pbs.at[other], pbr.at[kv], pb_sem, other, kv, (me, other))

    def pb_arrival(dk):
        other = lax.rem(kv + dk, n_kv)
        return remote(pbr.at[other], pbr.at[other], pb_sem, other, other, (me, other))

    for dk in range(1, n_kv):
        other = lax.rem(kv + dk, n_kv)
        for i in range(CHUNKS):
            relayed_w(dk, i).wait_recv()
        pbs[other] = dot(x_ref[...], wx[other])
        pb_copy(dk).start()
    for dk in range(1, n_kv):
        pb_arrival(dk).wait_recv()
    b_sum = pbr[0]
    for g in range(1, n_kv):
        b_sum = b_sum + pbr[g]
    b_all[blk(me)] = b_sum.astype(BF16)
    each(1, chips, lambda d: direct(b_all, b_sem, d).start())
    relay(b_all, br_sem, 0).start()
    pass_on(b_all, b_sem, br_sem)

    acc[...] = jnp.zeros_like(acc)

    def to_sib(i):
        return remote(
            db_all.at[i, pl.ds(pl.multiple_of((1 - core) * rows, rows), rows)], dbs.at[i], ds_sem, i, i, (sib, kv)
        )

    def to_owner(i):
        return remote(snd.at[i], arr.at[chip], da_sem, i, chip, (2 * i + core, kv))

    def from_chip(i):
        return remote(arr.at[i], arr.at[i], da_sem, i, i, (2 * i + core, kv))

    def joined(i):
        to_sib(i).wait_recv()
        return db_all[i, pl.ds(pl.multiple_of(core * rows, rows), rows)] + dbs[i]

    def send_on(i):
        snd[i] = joined(i).astype(BF16)
        to_owner(i).start()

    def residuals(t):
        i = lax.rem(chip + 1 + t, chips)
        b_two = b_all[blk(i, wide)]
        c_rows = c_st[...]
        student = dot(c_rows, b_two, NT)
        parts = []
        for u in range(2):
            part = student_scale * student[:, u * rows:(u + 1) * rows] - (
                s_buf[i, :, u * rows:(u + 1) * rows] * tot[...]
            )
            parts.append(jnp.where(seen(2 * i + u), part, 0.0).astype(BF16))
        resid = jnp.concatenate(parts, axis=1)
        db_all[i] = dot(resid, c_rows, TN)
        to_sib(i).start()
        acc[...] += dot(resid, b_two)

        @pl.when(t > 0)
        def _():
            send_on(lax.rem(chip + t, chips))

    each(0, chips, residuals)
    db_own[...] = joined(chip)
    for h in range(heads):
        gc_ref[:, h * width:(h + 1) * width] = acc[h * rows:(h + 1) * rows, :].astype(BF16)

    def take(d):
        i = lax.rem(chip + d, chips)
        from_chip(i).wait_recv()
        db_own[...] += arr[i].astype(F32)

    each(1, chips, take)
    dbg[kv, blk(pos)] = db_own[...].astype(BF16)

    def dg_target(d):
        idx = lax.rem(pos * n_kv + kv + d, per * n_kv)
        return idx, idx // n_kv, lax.rem(idx, n_kv)

    def dg_copy(d):
        idx, p, g = dg_target(d)
        spot = dbg.at[kv, blk(pos)]
        return remote(spot, spot, dg_sem, idx, pos * n_kv + kv, (grp * per + p, g))

    def dg_arrival(d):
        idx, p, g = dg_target(d)
        spot = dbg.at[g, blk(p)]
        return remote(spot, spot, dg_sem, idx, idx, (grp * per + p, g))

    each(1, per * n_kv, lambda d: dg_copy(d).start())
    each(1, per, lambda d: x_arrival(d).wait_recv())
    mine.wait()
    each(1, per * n_kv, lambda d: dg_arrival(d).wait_recv())

    owner = per * kv + pos

    def f_copy(g):
        return remote(fs.at[g], fr.at[grp], f_sem, g, grp, (owner, g))

    def f_arrival(h):
        return remote(fr.at[h], fr.at[h], f_sem, h, h, (h * per + pos, grp))

    for dk in range(n_kv):
        g = lax.rem(kv + 1 + dk, n_kv)
        part = dot(lt[...], dbg[g], TN)
        if dk < n_kv - 1:
            fs[g] = part.astype(BF16)
            f_copy(g).start()
        else:
            @pl.when(grp == kv)
            def _():
                gw_ref[0] = part

            @pl.when(grp != kv)
            def _():
                fs[g] = part.astype(BF16)
                f_copy(g).start()
                gw_ref[0] = jnp.zeros_like(part)

    for h in range(n_kv):
        @pl.when(jnp.logical_or(grp != kv, grp != h))
        def _():
            f_arrival(h).wait_recv()
            gw_ref[0] += fr[h].astype(F32)

    for i in range(CHUNKS):
        for dk in range(1, n_kv):
            w_copy(dk, i).wait_send()
            w_relay(dk, i).wait_send()
    for dk in range(1, n_kv):
        pb_copy(dk).wait_send()

    def drain(d):
        direct(k_all, k_sem, d).wait_send()
        direct(b_all, b_sem, d).wait_send()
        to_owner(lax.rem(chip + d, chips)).wait_send()

    def drain_all(d):
        relay(k_all, kr_sem, d).wait_send()
        relay(b_all, br_sem, d).wait_send()
        to_sib(d).wait_send()

    each(1, chips, drain)
    each(0, chips, drain_all)
    each(1, per, lambda d: x_copy(d).wait_send())
    each(1, per * n_kv, lambda d: dg_copy(d).wait_send())
    for g in range(n_kv):
        @pl.when(jnp.logical_or(grp != kv, kv != g))
        def _():
            f_copy(g).wait_send()


def local(n_seq, n_kv, plan, queries, keys, student_c, layer_input, b_weight):
    rows, width = keys.shape
    heads = queries.shape[1] // width
    half = layer_input.shape[1]
    depth = b_weight.shape[1]
    feat = depth // n_seq
    chips = n_seq // 2
    per = n_seq // n_kv
    stack = heads * rows
    vmem = pltpu.VMEM

    def pair(count):
        return pltpu.SemaphoreType.DMA((2, count))

    whole = pl.BlockSpec(memory_space=pltpu.VMEM)
    return pl.pallas_call(
        functools.partial(kernel, n_seq, n_kv, rows, width, heads),
        out_shape=(
            jax.ShapeDtypeStruct(queries.shape, BF16),
            jax.ShapeDtypeStruct((1, feat, width), F32),
        ),
        in_specs=[pl.BlockSpec(memory_space=pltpu.SMEM)] + [whole] * 5,
        out_specs=(whole, whole),
        scratch_shapes=[
            vmem((stack, width), BF16), vmem((stack, width), BF16),
            vmem((n_seq * rows, width), BF16), vmem((n_seq * rows, width), BF16),
            vmem((chips, stack, 2 * rows), F32),
            vmem((stack, rows), F32), vmem((stack, rows), F32), vmem((stack, width), F32),
            vmem((n_kv, half, width), BF16),
            vmem((n_kv, rows, width), F32), vmem((n_kv, rows, width), F32),
            vmem((per * rows, feat), BF16),
            vmem((chips, 2 * rows, width), F32), vmem((chips, rows, width), F32),
            vmem((chips, rows, width), BF16), vmem((chips, rows, width), BF16),
            vmem((rows, width), F32),
            vmem((n_kv, per * rows, width), BF16),
            vmem((n_kv, feat, width), BF16), vmem((n_kv, feat, width), BF16),
            pair(chips), pair(chips), pair(n_kv * CHUNKS), pair(n_kv * CHUNKS), pair(n_kv),
            pair(per), pair(chips), pair(chips), pair(chips), pair(chips), pair(per * n_kv),
            pair(n_kv), pltpu.SemaphoreType.DMA,
        ],
        compiler_params=pltpu.CompilerParams(
            collective_id=0, has_side_effects=True, vmem_limit_bytes=56 * 2**20
        ),
        name="ssm_grad",
    )(plan, queries, keys, student_c, layer_input, b_weight)


def solution(mesh):
    in_specs = (
        P(),
        P("seq", "kv"),
        P("seq", "kv"),
        P("seq", "kv"),
        P("seq", "kv"),
        P("kv", None, None),
    )
    out_specs = (P("seq", "kv"), P("kv", "seq", None))
    body = functools.partial(local, mesh.shape["seq"], mesh.shape["kv"])
    return jax.shard_map(body, mesh=mesh, in_specs=in_specs, out_specs=out_specs, check_vma=False)
```

```python
import functools
import math

import jax
import jax.numpy as jnp
from jax import lax
from jax.experimental import pallas as pl
from jax.experimental.pallas import tpu as pltpu
from jax.sharding import PartitionSpec as P

NEG_FILL = -1e30
MESH = pl.DeviceIdType.MESH
CHUNKS = 4
BF16 = jnp.bfloat16
F32 = jnp.float32
NT = (((1,), (1,)), ((), ()))
TN = (((0,), (0,)), ((), ()))


def dot(a, b, dims=(((1,), (0,)), ((), ()))):
    return lax.dot_general(a, b, dims, preferred_element_type=F32)


def kernel(
    n_seq, n_kv, rows, width, heads,
    plan, q_ref, k_ref, c_ref, x_any, w_any,
    gc_ref, gw_ref,
    x_ref, wv, q_t, c_t, c_st, k_all, b_all, s_buf, top, tot, acc,
    wx, pbs, pbr, lt, lt_t, db_all, dbs, snd, arr, db_own, dbg, fs, fr,
    k_sem, kr_sem, w_sem, wr_sem, pb_sem, x_sem, b_sem, br_sem, ds_sem, da_sem, dg_sem, dr_sem, f_sem, loc_sem,
):
    me, kv = lax.axis_index("seq"), lax.axis_index("kv")
    chips = n_seq // 2
    chip, core = me // 2, lax.rem(me, 2)
    sib = me + 1 - 2 * core
    per = n_seq // n_kv
    grp, pos = me // per, lax.rem(me, per)
    half = x_ref.shape[1]
    feat = half // per
    piece = half // 2
    step = piece // CHUNKS
    total = n_seq * n_kv
    wide = 2 * rows

    def blk(i, size=rows):
        return pl.ds(pl.multiple_of(i * size, size), size)

    def remote(src, dst, sems, i, j, dev):
        return pltpu.make_async_remote_copy(
            src_ref=src, dst_ref=dst, send_sem=sems.at[0, i], recv_sem=sems.at[1, j],
            device_id=dev, device_id_type=MESH,
        )

    barrier = pltpu.get_barrier_semaphore()
    flat = me * n_kv + kv

    def greet(d, carry):
        other = lax.rem(flat + d, total)
        pl.semaphore_signal(
            barrier, inc=1, device_id=(other // n_kv, lax.rem(other, n_kv)), device_id_type=MESH
        )
        return carry

    lax.fori_loop(1, total, greet, 0)
    own_half = pl.ds(pl.multiple_of(kv * half, half), half)
    load_x = pltpu.make_async_copy(x_any, x_ref, loc_sem.at[0])
    load_w = pltpu.make_async_copy(w_any.at[0, own_half], wv, loc_sem.at[1])
    load_x.start()
    load_w.start()
    pl.semaphore_wait(barrier, total - 1)

    def each(lo, hi, body):
        def run(i, carry):
            body(i)
            return carry

        lax.fori_loop(lo, hi, run, 0)

    def w_spot(other, part, i):
        return wx.at[other, pl.ds(pl.multiple_of(part * piece + i * step, step), step)]

    def w_copy(dk, i):
        other = lax.rem(kv + dk, n_kv)
        src = pl.ds(pl.multiple_of(other * half + core * piece + i * step, step), step)
        return remote(
            w_any.at[0, src], w_spot(kv, core, i), w_sem, other * CHUNKS + i, kv * CHUNKS + i, (me, other)
        )

    def w_hop(dk, i, part, sems, to):
        other = lax.rem(kv + dk, n_kv)
        spot = w_spot(other, part, i)
        return remote(spot, spot, sems, other * CHUNKS + i, other * CHUNKS + i, (to, kv))

    for i in range(CHUNKS):
        for dk in range(1, n_kv):
            w_copy(dk, i).start()

    def direct(buf, sems, d):
        to = lax.rem(chip + d, chips)
        spot = buf.at[blk(me)]
        return remote(spot, spot, sems, to, chip, (2 * to + core, kv))

    def arrival(buf, sems, d):
        frm = lax.rem(chip - d + chips, chips)
        spot = buf.at[blk(2 * frm + core)]
        return remote(spot, spot, sems, frm, frm, (2 * frm + core, kv))

    def relay(buf, sems, d):
        frm = lax.rem(chip - d + chips, chips)
        spot = buf.at[blk(2 * frm + core)]
        return remote(spot, spot, sems, frm, frm, (sib, kv))

    def relayed(buf, sems, d):
        frm = lax.rem(chip - d + chips, chips)
        spot = buf.at[blk(2 * frm + 1 - core)]
        return remote(spot, spot, sems, frm, frm, (sib, kv))

    def pass_on(buf, sems, rsems):
        def one(d):
            arrival(buf, sems, d).wait_recv()
            relay(buf, rsems, d).start()

        each(1, chips, one)
        each(0, chips, lambda d: relayed(buf, rsems, d).wait_recv())

    k_all[blk(me)] = k_ref[...]
    each(1, chips, lambda d: direct(k_all, k_sem, d).start())
    relay(k_all, kr_sem, 0).start()

    def x_copy(d):
        to = lax.rem(pos + d, per)
        cols = pl.ds(pl.multiple_of(to * feat, feat), feat)
        return remote(x_any.at[:, cols], lt.at[blk(pos)], x_sem, to, pos, (grp * per + to, kv))

    def x_arrival(d):
        frm = lax.rem(pos + d, per)
        spot = lt.at[blk(frm)]
        return remote(spot, spot, x_sem, frm, frm, (grp * per + frm, kv))

    each(1, per, lambda d: x_copy(d).start())
    own_cols = pl.ds(pl.multiple_of(pos * feat, feat), feat)
    mine = pltpu.make_async_copy(x_any.at[:, own_cols], lt.at[blk(pos)], loc_sem.at[2])
    mine.start()
    for h in range(heads):
        cols = slice(h * width, (h + 1) * width)
        q_t[:, h * rows:(h + 1) * rows] = q_ref[:, cols].astype(F32).T.astype(BF16)
        c_t[:, h * rows:(h + 1) * rows] = c_ref[:, cols].astype(F32).T.astype(BF16)
        c_st[h * rows:(h + 1) * rows, :] = c_ref[:, cols]
    load_x.wait()
    load_w.wait()
    pbr[kv] = dot(x_ref[...], wv[...])

    def w_forward(i):
        for dk in range(1, n_kv):
            w_hop(dk, i, core, w_sem, me).wait_recv()
            w_hop(dk, i, core, wr_sem, sib).start()

    pass_on(k_all, k_sem, kr_sem)
    w_forward(0)

    own_plan = plan[me]
    row_id = lax.broadcasted_iota(jnp.int32, (rows, heads * rows), 1)
    key_id = lax.broadcasted_iota(jnp.int32, (rows, heads * rows), 0)
    gap = key_id - lax.rem(row_id, rows)

    def seen(block):
        return gap <= (own_plan - plan[block]) * rows

    score_scale = 1.0 / math.sqrt(width)
    student_scale = 2.0 / math.sqrt(rows * n_seq)
    top[...] = jnp.full_like(top, NEG_FILL)

    def fold(part):
        return part.reshape(rows // 8, 8, heads * rows)

    def scores(i):
        both = dot(k_all[blk(i, wide)], q_t[...]) * score_scale
        high = top[...]
        for t in range(2):
            part = jnp.where(seen(2 * i + t), both[t * rows:(t + 1) * rows], NEG_FILL)
            s_buf[i, t * rows:(t + 1) * rows] = part
            high = jnp.maximum(high, jnp.max(fold(part), axis=0))
        top[...] = high

    each(0, chips, scores)
    w_forward(1)
    top[...] = jnp.broadcast_to(jnp.max(top[...], axis=0, keepdims=True), top.shape)

    def weights(i):
        added = tot[...]
        for t in range(2):
            part = jnp.exp(s_buf[i, t * rows:(t + 1) * rows] - top[0:1])
            s_buf[i, t * rows:(t + 1) * rows] = part
            added = added + jnp.sum(fold(part), axis=0)
        tot[...] = added

    tot[...] = jnp.zeros_like(tot)
    each(0, chips, weights)
    tot[...] = jnp.broadcast_to(1.0 / jnp.sum(tot[...], axis=0, keepdims=True), tot.shape)
    for i in range(2, CHUNKS):
        w_forward(i)

    def pb_copy(dk):
        other = lax.rem(kv + dk, n_kv)
        return remote(pbs.at[other], pbr.at[kv], pb_sem, other, kv, (me, other))

    def pb_arrival(dk):
        other = lax.rem(kv + dk, n_kv)
        return remote(pbr.at[other], pbr.at[other], pb_sem, other, other, (me, other))

    for dk in range(1, n_kv):
        other = lax.rem(kv + dk, n_kv)
        for i in range(CHUNKS):
            w_hop(dk, i, 1 - core, wr_sem, sib).wait_recv()
        pbs[other] = dot(x_ref[...], wx[other])
        pb_copy(dk).start()
    for dk in range(1, n_kv):
        pb_arrival(dk).wait_recv()
    b_sum = pbr[0]
    for g in range(1, n_kv):
        b_sum = b_sum + pbr[g]
    b_all[blk(me)] = b_sum.astype(BF16)
    each(1, chips, lambda d: direct(b_all, b_sem, d).start())
    relay(b_all, br_sem, 0).start()

    acc[...] = jnp.zeros_like(acc)

    def to_sib(i):
        return remote(
            db_all.at[i, pl.ds(pl.multiple_of((1 - core) * rows, rows), rows)], dbs.at[i], ds_sem, i, i, (sib, kv)
        )

    def to_owner(i):
        return remote(snd.at[i], arr.at[chip], da_sem, i, chip, (2 * i + core, kv))

    def from_chip(i):
        return remote(arr.at[i], arr.at[i], da_sem, i, i, (2 * i + core, kv))

    def joined(i):
        to_sib(i).wait_recv()
        return db_all[i, pl.ds(pl.multiple_of(core * rows, rows), rows)] + dbs[i]

    def send_on(i):
        snd[i] = joined(i).astype(BF16)
        to_owner(i).start()

    def residuals(t):
        i = lax.rem(chip - t + chips, chips)

        @pl.when(t < chips - 1)
        def _():
            arrival(b_all, b_sem, t + 1).wait_recv()
            relay(b_all, br_sem, t + 1).start()

        relayed(b_all, br_sem, t).wait_recv()
        b_two = b_all[blk(i, wide)]
        student = dot(b_two, c_t[...])
        parts = []
        for u in range(2):
            part = student_scale * student[u * rows:(u + 1) * rows] - (
                s_buf[i, u * rows:(u + 1) * rows] * tot[0:1]
            )
            parts.append(jnp.where(seen(2 * i + u), part, 0.0).astype(BF16))
        resid = jnp.concatenate(parts, axis=0)
        db_all[i] = dot(resid, c_st[...])
        to_sib(i).start()
        acc[...] += dot(b_two, resid, TN)

        @pl.when(t > 1)
        def _():
            send_on(lax.rem(chip - t + 1 + chips, chips))

    each(0, chips, residuals)
    send_on(lax.rem(chip + 1, chips))
    db_own[...] = joined(chip)
    for h in range(heads):
        gc_ref[:, h * width:(h + 1) * width] = acc[:, h * rows:(h + 1) * rows].T.astype(BF16)
    each(1, per, lambda d: x_arrival(d).wait_recv())
    mine.wait()

    def turn(p):
        lt_t[:, blk(p)] = lt[blk(p)].T

    each(0, per, turn)

    def take(d):
        i = lax.rem(chip + d, chips)
        from_chip(i).wait_recv()
        db_own[...] += arr[i].astype(F32)

    each(1, chips, take)
    dbg[kv, blk(pos)] = db_own[...].astype(BF16)

    count = per // 2 * n_kv
    spot_own = pos // 2 * n_kv + kv

    def dg_at(idx, which):
        return dbg.at[lax.rem(idx, n_kv), blk(2 * (idx // n_kv) + which)]

    def dg_copy(d):
        to = lax.rem(spot_own + d, count)
        spot = dg_at(spot_own, core)
        return remote(spot, spot, dg_sem, to, spot_own, (grp * per + 2 * (to // n_kv) + core, lax.rem(to, n_kv)))

    def dg_hop(d, sems, which):
        frm = lax.rem(spot_own - d + count, count)
        spot = dg_at(frm, which)
        return remote(spot, spot, sems, frm, frm, (sib, kv))

    each(1, count, lambda d: dg_copy(d).start())
    dg_hop(0, dr_sem, core).start()

    def dg_pass(d):
        dg_hop(d, dg_sem, core).wait_recv()
        dg_hop(d, dr_sem, core).start()

    each(1, count, dg_pass)
    each(0, count, lambda d: dg_hop(d, dr_sem, 1 - core).wait_recv())

    owner = per * kv + pos

    def f_copy(g):
        return remote(fs.at[g], fr.at[grp], f_sem, g, grp, (owner, g))

    def f_arrival(h):
        return remote(fr.at[h], fr.at[h], f_sem, h, h, (h * per + pos, grp))

    for dk in range(n_kv):
        g = lax.rem(kv + 1 + dk, n_kv)
        part = dot(lt_t[...], dbg[g])
        if dk < n_kv - 1:
            fs[g] = part.astype(BF16)
            f_copy(g).start()
        else:
            @pl.when(grp == kv)
            def _():
                gw_ref[0] = part

            @pl.when(grp != kv)
            def _():
                fs[g] = part.astype(BF16)
                f_copy(g).start()
                gw_ref[0] = jnp.zeros_like(part)

    for h in range(n_kv):
        @pl.when(jnp.logical_or(grp != kv, grp != h))
        def _():
            f_arrival(h).wait_recv()
            gw_ref[0] += fr[h].astype(F32)

    for i in range(CHUNKS):
        for dk in range(1, n_kv):
            w_copy(dk, i).wait_send()
            w_hop(dk, i, core, wr_sem, sib).wait_send()
    for dk in range(1, n_kv):
        pb_copy(dk).wait_send()

    def drain(d):
        direct(k_all, k_sem, d).wait_send()
        direct(b_all, b_sem, d).wait_send()
        to_owner(lax.rem(chip + d, chips)).wait_send()

    def drain_all(d):
        relay(k_all, kr_sem, d).wait_send()
        relay(b_all, br_sem, d).wait_send()
        to_sib(d).wait_send()

    each(1, chips, drain)
    each(0, chips, drain_all)
    each(1, per, lambda d: x_copy(d).wait_send())
    each(1, count, lambda d: dg_copy(d).wait_send())
    each(0, count, lambda d: dg_hop(d, dr_sem, core).wait_send())
    for g in range(n_kv):
        @pl.when(jnp.logical_or(grp != kv, kv != g))
        def _():
            f_copy(g).wait_send()


def local(n_seq, n_kv, plan, queries, keys, student_c, layer_input, b_weight):
    rows, width = keys.shape
    heads = queries.shape[1] // width
    half = layer_input.shape[1]
    depth = b_weight.shape[1]
    feat = depth // n_seq
    chips = n_seq // 2
    per = n_seq // n_kv
    stack = heads * rows
    vmem = pltpu.VMEM

    def pair(count):
        return pltpu.SemaphoreType.DMA((2, count))

    whole = pl.BlockSpec(memory_space=pltpu.VMEM)
    return pl.pallas_call(
        functools.partial(kernel, n_seq, n_kv, rows, width, heads),
        out_shape=(
            jax.ShapeDtypeStruct(queries.shape, BF16),
            jax.ShapeDtypeStruct((1, feat, width), F32),
        ),
        in_specs=[pl.BlockSpec(memory_space=pltpu.SMEM)] + [whole] * 3 + [pl.BlockSpec(memory_space=pl.ANY)] * 2,
        out_specs=(whole, whole),
        scratch_shapes=[
            vmem((rows, half), BF16), vmem((half, width), BF16),
            vmem((width, stack), BF16), vmem((width, stack), BF16), vmem((stack, width), BF16),
            vmem((n_seq * rows, width), BF16), vmem((n_seq * rows, width), BF16),
            vmem((chips, 2 * rows, stack), F32),
            vmem((8, stack), F32), vmem((8, stack), F32), vmem((width, stack), F32),
            vmem((n_kv, half, width), BF16),
            vmem((n_kv, rows, width), F32), vmem((n_kv, rows, width), F32),
            vmem((per * rows, feat), BF16), vmem((feat, per * rows), BF16),
            vmem((chips, 2 * rows, width), F32), vmem((chips, rows, width), F32),
            vmem((chips, rows, width), BF16), vmem((chips, rows, width), BF16),
            vmem((rows, width), F32),
            vmem((n_kv, per * rows, width), BF16),
            vmem((n_kv, feat, width), BF16), vmem((n_kv, feat, width), BF16),
            pair(chips), pair(chips), pair(n_kv * CHUNKS), pair(n_kv * CHUNKS), pair(n_kv),
            pair(per), pair(chips), pair(chips), pair(chips), pair(chips), pair(per // 2 * n_kv),
            pair(per // 2 * n_kv), pair(n_kv), pltpu.SemaphoreType.DMA((3,)),
        ],
        compiler_params=pltpu.CompilerParams(
            collective_id=0, has_side_effects=True, vmem_limit_bytes=56 * 2**20
        ),
        name="ssm_grad",
    )(plan, queries, keys, student_c, layer_input, b_weight)


def solution(mesh):
    in_specs = (
        P(),
        P("seq", "kv"),
        P("seq", "kv"),
        P("seq", "kv"),
        P("seq", "kv"),
        P("kv", None, None),
    )
    out_specs = (P("seq", "kv"), P("kv", "seq", None))
    body = functools.partial(local, mesh.shape["seq"], mesh.shape["kv"])
    return jax.shard_map(body, mesh=mesh, in_specs=in_specs, out_specs=out_specs, check_vma=False)
```

```python
import functools
import math

import jax
import jax.numpy as jnp
from jax import lax
from jax.experimental import pallas as pl
from jax.experimental.pallas import tpu as pltpu
from jax.sharding import PartitionSpec as P

NEG_FILL = -1e30
MESH = pl.DeviceIdType.MESH
CHUNKS = 4
PARTS = 4
BF16 = jnp.bfloat16
F32 = jnp.float32
NT = (((1,), (1,)), ((), ()))
TN = (((0,), (0,)), ((), ()))


def dot(a, b, dims=(((1,), (0,)), ((), ()))):
    return lax.dot_general(a, b, dims, preferred_element_type=F32)


def kernel(
    n_seq, n_kv, rows, width, heads,
    plan, q_ref, k_ref, c_ref, x_any, w_any,
    gc_ref, gw_ref,
    x_ref, wv, q_t, c_t, c_st, k_all, b_all, s_buf, top, tot, acc,
    wx, pbs, pbr, lt, lt_t, db_all, dbs, snd, arr, db_own, dbg, fs, fx, fr,
    k_sem, kr_sem, w_sem, wr_sem, pb_sem, x_sem, b_sem, br_sem, ds_sem, da_sem, dg_sem, dr_sem, f_sem, fa_sem, loc_sem,
):
    me, kv = lax.axis_index("seq"), lax.axis_index("kv")
    chips = n_seq // 2
    chip, core = me // 2, lax.rem(me, 2)
    sib = me + 1 - 2 * core
    per = n_seq // n_kv
    grp, pos = me // per, lax.rem(me, per)
    half = x_ref.shape[1]
    feat = half // per
    piece = half // 2
    step = piece // CHUNKS
    total = n_seq * n_kv
    wide = 2 * rows

    def blk(i, size=rows):
        return pl.ds(pl.multiple_of(i * size, size), size)

    def remote(src, dst, sems, i, j, dev):
        return pltpu.make_async_remote_copy(
            src_ref=src, dst_ref=dst, send_sem=sems.at[0, i], recv_sem=sems.at[1, j],
            device_id=dev, device_id_type=MESH,
        )

    barrier = pltpu.get_barrier_semaphore()
    flat = me * n_kv + kv

    def greet(d, carry):
        other = lax.rem(flat + d, total)
        pl.semaphore_signal(
            barrier, inc=1, device_id=(other // n_kv, lax.rem(other, n_kv)), device_id_type=MESH
        )
        return carry

    lax.fori_loop(1, total, greet, 0)
    own_half = pl.ds(pl.multiple_of(kv * half, half), half)
    load_x = pltpu.make_async_copy(x_any, x_ref, loc_sem.at[0])
    load_w = pltpu.make_async_copy(w_any.at[0, own_half], wv, loc_sem.at[1])
    load_x.start()
    load_w.start()
    pl.semaphore_wait(barrier, total - 1)

    def each(lo, hi, body):
        def run(i, carry):
            body(i)
            return carry

        lax.fori_loop(lo, hi, run, 0)

    def w_spot(other, part, i):
        return wx.at[other, pl.ds(pl.multiple_of(part * piece + i * step, step), step)]

    def w_copy(dk, i):
        other = lax.rem(kv + dk, n_kv)
        src = pl.ds(pl.multiple_of(other * half + core * piece + i * step, step), step)
        return remote(
            w_any.at[0, src], w_spot(kv, core, i), w_sem, other * CHUNKS + i, kv * CHUNKS + i, (me, other)
        )

    def w_hop(dk, i, part, sems, to):
        other = lax.rem(kv + dk, n_kv)
        spot = w_spot(other, part, i)
        return remote(spot, spot, sems, other * CHUNKS + i, other * CHUNKS + i, (to, kv))

    for i in range(CHUNKS):
        for dk in range(1, n_kv):
            w_copy(dk, i).start()

    def direct(buf, sems, d):
        to = lax.rem(chip + d, chips)
        spot = buf.at[blk(me)]
        return remote(spot, spot, sems, to, chip, (2 * to + core, kv))

    def arrival(buf, sems, d):
        frm = lax.rem(chip - d + chips, chips)
        spot = buf.at[blk(2 * frm + core)]
        return remote(spot, spot, sems, frm, frm, (2 * frm + core, kv))

    def relay(buf, sems, d):
        frm = lax.rem(chip - d + chips, chips)
        spot = buf.at[blk(2 * frm + core)]
        return remote(spot, spot, sems, frm, frm, (sib, kv))

    def relayed(buf, sems, d):
        frm = lax.rem(chip - d + chips, chips)
        spot = buf.at[blk(2 * frm + 1 - core)]
        return remote(spot, spot, sems, frm, frm, (sib, kv))

    def pass_on(buf, sems, rsems):
        def one(d):
            arrival(buf, sems, d).wait_recv()
            relay(buf, rsems, d).start()

        each(1, chips, one)
        each(0, chips, lambda d: relayed(buf, rsems, d).wait_recv())

    k_all[blk(me)] = k_ref[...]
    each(1, chips, lambda d: direct(k_all, k_sem, d).start())
    relay(k_all, kr_sem, 0).start()

    def x_copy(d):
        to = lax.rem(pos + d, per)
        cols = pl.ds(pl.multiple_of(to * feat, feat), feat)
        return remote(x_any.at[:, cols], lt.at[blk(pos)], x_sem, to, pos, (grp * per + to, kv))

    def x_arrival(d):
        frm = lax.rem(pos + d, per)
        spot = lt.at[blk(frm)]
        return remote(spot, spot, x_sem, frm, frm, (grp * per + frm, kv))

    each(1, per, lambda d: x_copy(d).start())
    own_cols = pl.ds(pl.multiple_of(pos * feat, feat), feat)
    mine = pltpu.make_async_copy(x_any.at[:, own_cols], lt.at[blk(pos)], loc_sem.at[2])
    mine.start()
    for h in range(heads):
        cols = slice(h * width, (h + 1) * width)
        q_t[:, h * rows:(h + 1) * rows] = q_ref[:, cols].astype(F32).T.astype(BF16)
        c_t[:, h * rows:(h + 1) * rows] = c_ref[:, cols].astype(F32).T.astype(BF16)
        c_st[h * rows:(h + 1) * rows, :] = c_ref[:, cols]
    load_x.wait()
    load_w.wait()
    pbr[kv] = dot(x_ref[...], wv[...])

    def w_forward(i):
        for dk in range(1, n_kv):
            w_hop(dk, i, core, w_sem, me).wait_recv()
            w_hop(dk, i, core, wr_sem, sib).start()

    pass_on(k_all, k_sem, kr_sem)
    w_forward(0)

    own_plan = plan[me]
    row_id = lax.broadcasted_iota(jnp.int32, (rows, heads * rows), 1)
    key_id = lax.broadcasted_iota(jnp.int32, (rows, heads * rows), 0)
    gap = key_id - lax.rem(row_id, rows)

    def seen(block):
        return gap <= (own_plan - plan[block]) * rows

    score_scale = 1.0 / math.sqrt(width)
    student_scale = 2.0 / math.sqrt(rows * n_seq)
    top[...] = jnp.full_like(top, NEG_FILL)

    def fold(part):
        return part.reshape(rows // 8, 8, heads * rows)

    def scores(i):
        both = dot(k_all[blk(i, wide)], q_t[...]) * score_scale
        high = top[...]
        for t in range(2):
            part = jnp.where(seen(2 * i + t), both[t * rows:(t + 1) * rows], NEG_FILL)
            s_buf[i, t * rows:(t + 1) * rows] = part
            high = jnp.maximum(high, jnp.max(fold(part), axis=0))
        top[...] = high

    each(0, chips, scores)
    w_forward(1)
    top[...] = jnp.broadcast_to(jnp.max(top[...], axis=0, keepdims=True), top.shape)

    def weights(i):
        added = tot[...]
        for t in range(2):
            part = jnp.exp(s_buf[i, t * rows:(t + 1) * rows] - top[0:1])
            s_buf[i, t * rows:(t + 1) * rows] = part
            added = added + jnp.sum(fold(part), axis=0)
        tot[...] = added

    tot[...] = jnp.zeros_like(tot)
    each(0, chips, weights)
    tot[...] = jnp.broadcast_to(1.0 / jnp.sum(tot[...], axis=0, keepdims=True), tot.shape)
    for i in range(2, CHUNKS):
        w_forward(i)

    def pb_copy(dk):
        other = lax.rem(kv + dk, n_kv)
        return remote(pbs.at[other], pbr.at[kv], pb_sem, other, kv, (me, other))

    def pb_arrival(dk):
        other = lax.rem(kv + dk, n_kv)
        return remote(pbr.at[other], pbr.at[other], pb_sem, other, other, (me, other))

    for dk in range(1, n_kv):
        other = lax.rem(kv + dk, n_kv)
        for i in range(CHUNKS):
            w_hop(dk, i, 1 - core, wr_sem, sib).wait_recv()
        pbs[other] = dot(x_ref[...], wx[other])
        pb_copy(dk).start()
    for dk in range(1, n_kv):
        pb_arrival(dk).wait_recv()
    b_sum = pbr[0]
    for g in range(1, n_kv):
        b_sum = b_sum + pbr[g]
    b_all[blk(me)] = b_sum.astype(BF16)
    each(1, chips, lambda d: direct(b_all, b_sem, d).start())
    relay(b_all, br_sem, 0).start()

    acc[...] = jnp.zeros_like(acc)

    def to_sib(i):
        return remote(
            db_all.at[i, pl.ds(pl.multiple_of((1 - core) * rows, rows), rows)], dbs.at[i], ds_sem, i, i, (sib, kv)
        )

    def to_owner(i):
        return remote(snd.at[i], arr.at[chip], da_sem, i, chip, (2 * i + core, kv))

    def from_chip(i):
        return remote(arr.at[i], arr.at[i], da_sem, i, i, (2 * i + core, kv))

    def joined(i):
        to_sib(i).wait_recv()
        return db_all[i, pl.ds(pl.multiple_of(core * rows, rows), rows)] + dbs[i]

    def send_on(i):
        snd[i] = joined(i).astype(BF16)
        to_owner(i).start()

    def residuals(t):
        i = lax.rem(chip - t + chips, chips)

        @pl.when(t < chips - 1)
        def _():
            arrival(b_all, b_sem, t + 1).wait_recv()
            relay(b_all, br_sem, t + 1).start()

        relayed(b_all, br_sem, t).wait_recv()
        b_two = b_all[blk(i, wide)]
        student = dot(b_two, c_t[...])
        parts = []
        for u in range(2):
            part = student_scale * student[u * rows:(u + 1) * rows] - (
                s_buf[i, u * rows:(u + 1) * rows] * tot[0:1]
            )
            parts.append(jnp.where(seen(2 * i + u), part, 0.0).astype(BF16))
        resid = jnp.concatenate(parts, axis=0)
        db_all[i] = dot(resid, c_st[...])
        to_sib(i).start()
        acc[...] += dot(b_two, resid, TN)

        @pl.when(t > 1)
        def _():
            send_on(lax.rem(chip - t + 1 + chips, chips))

    each(0, chips, residuals)
    send_on(lax.rem(chip + 1, chips))
    db_own[...] = joined(chip)
    for h in range(heads):
        gc_ref[:, h * width:(h + 1) * width] = acc[:, h * rows:(h + 1) * rows].T.astype(BF16)
    each(1, per, lambda d: x_arrival(d).wait_recv())
    mine.wait()

    def turn(p):
        lt_t[:, blk(p)] = lt[blk(p)].T

    each(0, per, turn)

    def take(d):
        i = lax.rem(chip + d, chips)
        from_chip(i).wait_recv()
        db_own[...] += arr[i].astype(F32)

    each(1, chips, take)
    dbg[kv, blk(pos)] = db_own[...].astype(BF16)

    count = per // 2 * n_kv
    spot_own = pos // 2 * n_kv + kv

    def dg_at(idx, which):
        return dbg.at[lax.rem(idx, n_kv), blk(2 * (idx // n_kv) + which)]

    def dg_copy(d):
        to = lax.rem(spot_own + d, count)
        spot = dg_at(spot_own, core)
        return remote(spot, spot, dg_sem, to, spot_own, (grp * per + 2 * (to // n_kv) + core, lax.rem(to, n_kv)))

    def dg_hop(d, sems, which):
        frm = lax.rem(spot_own - d + count, count)
        spot = dg_at(frm, which)
        return remote(spot, spot, sems, frm, frm, (sib, kv))

    each(1, count, lambda d: dg_copy(d).start())
    dg_hop(0, dr_sem, core).start()

    def dg_pass(d):
        dg_hop(d, dg_sem, core).wait_recv()
        dg_hop(d, dr_sem, core).start()

    each(1, count, dg_pass)
    each(0, count, lambda d: dg_hop(d, dr_sem, 1 - core).wait_recv())

    part_rows = feat // PARTS

    def f_rows(u):
        return pl.ds(u * part_rows, part_rows)

    def f_cross(g, u):
        return remote(
            fs.at[g, f_rows(u)], fx.at[kv, f_rows(u)], f_sem, g * PARTS + u, kv * PARTS + u, (me, g)
        )

    def f_crossed(g, u):
        spot = fx.at[g, f_rows(u)]
        return remote(spot, spot, f_sem, g * PARTS + u, g * PARTS + u, (me, g))

    def f_along(buf, k, u):
        return remote(
            buf.at[k, f_rows(u)], fr.at[grp, f_rows(u)], fa_sem, k * PARTS + u, grp * PARTS + u, (per * k + pos, kv)
        )

    def f_arrival(h, u):
        spot = fr.at[h, f_rows(u)]
        return remote(spot, spot, fa_sem, h * PARTS + u, h * PARTS + u, (h * per + pos, kv))

    for u in range(PARTS):
        for dk in range(1, n_kv):
            g = lax.rem(kv + dk, n_kv)
            fs[g, f_rows(u)] = dot(lt_t[f_rows(u)], dbg[g]).astype(BF16)
            f_cross(g, u).start()
    part = dot(lt_t[...], dbg[kv])

    @pl.when(grp == kv)
    def _():
        gw_ref[0] = part

    @pl.when(grp != kv)
    def _():
        fs[kv] = part.astype(BF16)
        for u in range(PARTS):
            f_along(fs, kv, u).start()
        gw_ref[0] = jnp.zeros_like(part)

    for u in range(PARTS):
        for dk in range(1, n_kv):
            g = lax.rem(kv + dk, n_kv)
            f_crossed(g, u).wait_recv()

            @pl.when(grp == g)
            def _():
                gw_ref[0, f_rows(u)] += fx[g, f_rows(u)].astype(F32)

            @pl.when(grp != g)
            def _():
                f_along(fx, g, u).start()

    for u in range(PARTS):
        for dk in range(1, n_kv):
            h = lax.rem(grp + dk, n_kv)
            f_arrival(h, u).wait_recv()
            gw_ref[0, f_rows(u)] += fr[h, f_rows(u)].astype(F32)

    for i in range(CHUNKS):
        for dk in range(1, n_kv):
            w_copy(dk, i).wait_send()
            w_hop(dk, i, core, wr_sem, sib).wait_send()
    for dk in range(1, n_kv):
        pb_copy(dk).wait_send()

    def drain(d):
        direct(k_all, k_sem, d).wait_send()
        direct(b_all, b_sem, d).wait_send()
        to_owner(lax.rem(chip + d, chips)).wait_send()

    def drain_all(d):
        relay(k_all, kr_sem, d).wait_send()
        relay(b_all, br_sem, d).wait_send()
        to_sib(d).wait_send()

    each(1, chips, drain)
    each(0, chips, drain_all)
    each(1, per, lambda d: x_copy(d).wait_send())
    each(1, count, lambda d: dg_copy(d).wait_send())
    each(0, count, lambda d: dg_hop(d, dr_sem, core).wait_send())
    for dk in range(1, n_kv):
        for u in range(PARTS):
            f_cross(lax.rem(kv + dk, n_kv), u).wait_send()
            f_along(fx, lax.rem(grp + dk, n_kv), u).wait_send()


def local(n_seq, n_kv, plan, queries, keys, student_c, layer_input, b_weight):
    rows, width = keys.shape
    heads = queries.shape[1] // width
    half = layer_input.shape[1]
    depth = b_weight.shape[1]
    feat = depth // n_seq
    chips = n_seq // 2
    per = n_seq // n_kv
    stack = heads * rows
    vmem = pltpu.VMEM

    def pair(count):
        return pltpu.SemaphoreType.DMA((2, count))

    whole = pl.BlockSpec(memory_space=pltpu.VMEM)
    return pl.pallas_call(
        functools.partial(kernel, n_seq, n_kv, rows, width, heads),
        out_shape=(
            jax.ShapeDtypeStruct(queries.shape, BF16),
            jax.ShapeDtypeStruct((1, feat, width), F32),
        ),
        in_specs=[pl.BlockSpec(memory_space=pltpu.SMEM)] + [whole] * 3 + [pl.BlockSpec(memory_space=pl.ANY)] * 2,
        out_specs=(whole, whole),
        scratch_shapes=[
            vmem((rows, half), BF16), vmem((half, width), BF16),
            vmem((width, stack), BF16), vmem((width, stack), BF16), vmem((stack, width), BF16),
            vmem((n_seq * rows, width), BF16), vmem((n_seq * rows, width), BF16),
            vmem((chips, 2 * rows, stack), F32),
            vmem((8, stack), F32), vmem((8, stack), F32), vmem((width, stack), F32),
            vmem((n_kv, half, width), BF16),
            vmem((n_kv, rows, width), F32), vmem((n_kv, rows, width), F32),
            vmem((per * rows, feat), BF16), vmem((feat, per * rows), BF16),
            vmem((chips, 2 * rows, width), F32), vmem((chips, rows, width), F32),
            vmem((chips, rows, width), BF16), vmem((chips, rows, width), BF16),
            vmem((rows, width), F32),
            vmem((n_kv, per * rows, width), BF16),
            vmem((n_kv, feat, width), BF16), vmem((n_kv, feat, width), BF16), vmem((n_kv, feat, width), BF16),
            pair(chips), pair(chips), pair(n_kv * CHUNKS), pair(n_kv * CHUNKS), pair(n_kv),
            pair(per), pair(chips), pair(chips), pair(chips), pair(chips), pair(per // 2 * n_kv),
            pair(per // 2 * n_kv), pair(n_kv * PARTS), pair(n_kv * PARTS), pltpu.SemaphoreType.DMA((3,)),
        ],
        compiler_params=pltpu.CompilerParams(
            collective_id=0, has_side_effects=True, vmem_limit_bytes=56 * 2**20
        ),
        name="ssm_grad",
    )(plan, queries, keys, student_c, layer_input, b_weight)


def solution(mesh):
    in_specs = (
        P(),
        P("seq", "kv"),
        P("seq", "kv"),
        P("seq", "kv"),
        P("seq", "kv"),
        P("kv", None, None),
    )
    out_specs = (P("seq", "kv"), P("kv", "seq", None))
    body = functools.partial(local, mesh.shape["seq"], mesh.shape["kv"])
    return jax.shard_map(body, mesh=mesh, in_specs=in_specs, out_specs=out_specs, check_vma=False)
```
